32 devices in a mesh: groups: 2 (over x), tile: 8 (over z, y), freq: 2 (over core).
Axes of the slice: x: 2, y: 2, z: 4, core: 2. Of those that a mesh axis runs over, the one named last changes fastest.
Arguments:
- panels: bfloat16 [8, 2, 256, 384], P('freq'), may hold values from -0.3125 to 0.3125
- snapshots: bfloat16 [16, 2, 32, 256], P(('groups', 'freq')), parts along dimension 0, may hold values from -6 to 6
- wavenumbers: float32 [8, 384], P('freq'), may hold values from 0.05 to 0.5
- mode_counts: int32 [8], P('freq'), may hold values from 48 to 384, as said below
- mode_mask: int32 [8, 3, 64], P('freq'), may hold values from 0 to 1, as said below
- mode_shapes: bfloat16 [8, 2048, 384], P('freq', 'tile'), may hold values from -6 to 6
Outputs:
- surface: float32 [32, 2048], P(('groups', 'tile', 'freq')), parts along dimension 0
The draws below stay inside these ranges and needn't reach their ends.
There are 2 independent parts, one for each index of `groups`. The reference program is written for one: setup_inputs(seed, part) draws one part's arguments, and reference() takes and returns one part's arrays. A program takes and returns all parts, laid end to end along the dimension named above; an argument that names none is the same for every part. Nothing has to cross between parts.
Inputs may be any that keep to these rules, and one draw needn't show every extreme that they name: `mode_counts`: some frequency has exactly 384 modes and some exactly 48. `mode_mask`: mode block 0 is live in every depth block of every frequency.
All inputs are finite; a program needn't handle non-finite values.
Results may differ from the reference program's by a relative error of at most 0.0005.
Values may be sent and summed in bfloat16 or wider, within the bound.
A program may use at most 64 MiB of HBM per device.

```python
import math
import jax
import jax.numpy as jnp
from jax import lax

M = 256
KMAX = 384
KMIN = 48
MBLK = 128
ZBLK = 32
SNAPS = 32
DEPTHS = 2048
FREQS = 8
RANGES = 16
MODE_BLOCKS = 3
DEPTH_BLOCKS = 64


def draw_mode_counts(key, part):
    key_values, key_top, key_low = jax.random.split(key, 3)
    values = jax.random.randint(key_values, (FREQS,), KMIN, KMAX + 1)
    top_slot = jax.random.randint(key_top, (), 0, FREQS)
    low_slot = (top_slot + 1 + jax.random.randint(key_low, (), 0, FREQS - 1)) % FREQS
    positions = jnp.arange(FREQS)
    values = jnp.where(positions == top_slot, KMAX, values)
    values = jnp.where(positions == low_slot, KMIN, values)
    return values.astype(jnp.int32)


def draw_mode_mask(key, part):
    random_bits = jax.random.randint(key, (FREQS, MODE_BLOCKS, DEPTH_BLOCKS), 0, 2)
    block_index = jnp.arange(MODE_BLOCKS)[None, :, None]
    return jnp.where(block_index == 0, 1, random_bits).astype(jnp.int32)


def block_levels(own_key, shape, cuts, least, largest):
    gain, own = 1.0, jax.random.fold_in(own_key, 6)
    for position, parts in cuts:
        heights = jnp.exp(jax.random.uniform(jax.random.fold_in(own, position), (parts,), jnp.float32, least / len(cuts), largest / len(cuts)))
        gain = gain * jnp.repeat(heights, shape[position] // parts).reshape([-1 if axis == position else 1 for axis in range(len(shape))])
    return gain


def gaussian(own_key, shape, scale, most, cuts=(), held_as=jnp.bfloat16):
    entries = jax.random.normal(own_key, shape, jnp.float32) * scale
    if len(cuts) > 0:
        entries = block_levels(own_key, shape, cuts, -0.22, 0.18) * entries
    return jnp.clip(entries, min=-most, max=most).astype(held_as)


def setup_inputs(seed: int = 0, part: int = 0) -> dict:
    splits = jax.random.split(jax.random.key(seed), 7)
    part_splits = jax.random.split(jax.random.fold_in(splits[6], part), 7)
    return {
        "panels": gaussian(splits[0], (FREQS, 2, M, KMAX), KMAX ** -0.5, 0.3125, ((0, 2),)),
        "snapshots": gaussian(part_splits[1], (FREQS, 2, SNAPS, M), 1.0, 6.0, ((0, 2),)),
        "wavenumbers": jnp.clip(jnp.exp(math.log(0.5) - 2.3025851 * jax.random.uniform(splits[2], (FREQS, KMAX), jnp.float32) ** block_levels(splits[2], (FREQS, KMAX), ((0, 2),), -0.2, 0.2)), 0.05, 0.5),
        "mode_counts": draw_mode_counts(jax.random.fold_in(splits[6], 71), part),
        "mode_mask": draw_mode_mask(jax.random.fold_in(splits[6], 71), part),
        "mode_shapes": gaussian(splits[5], (FREQS, DEPTHS, KMAX), 1.0, 6.0, ((0, 2), (1, 8))),
    }


range_anchor = 1000.0
range_step = 25.0


def block_power(shapes, first_depth, first_range, range_count, panels, snapshots, wavenumbers, mode_counts, mode_mask):
    depth_count = shapes.shape[1]
    modes = shapes.shape[2]
    receivers = panels.shape[2]
    snap_count = snapshots.shape[2]
    block_count = mode_mask.shape[2]
    depth_index = first_depth + jnp.arange(depth_count, dtype=jnp.int32)
    depth_onehot = ((depth_index[:, None] // ZBLK) == jnp.arange(block_count, dtype=jnp.int32)[None, :]).astype(jnp.float32)
    distances = range_anchor + range_step * (first_range + jnp.arange(range_count, dtype=jnp.int32)).astype(jnp.float32)
    mode_index = jnp.arange(modes, dtype=jnp.int32)

    def one_freq(totals, inputs):
        shape_rows, panel_pair, snap_pair, wavenumber, mode_count, live_blocks = inputs
        depth_live = jnp.dot(depth_onehot, live_blocks.astype(jnp.float32).T)
        live_modes = jnp.repeat(depth_live, MBLK, axis=1) * (mode_index < mode_count).astype(jnp.float32)[None, :]
        shaped = shape_rows.astype(jnp.float32) * live_modes
        phases = distances[:, None] * wavenumber[None, :]
        real_part = (jnp.cos(phases)[:, None, :] * shaped[None, :, :]).reshape(-1, modes)
        imag_part = (jnp.sin(phases)[:, None, :] * shaped[None, :, :]).reshape(-1, modes)
        mode_terms = jnp.concatenate([real_part, imag_part], axis=1).astype(jnp.bfloat16)
        stacked = jnp.concatenate([jnp.concatenate([panel_pair[0], -panel_pair[1]], axis=1),
                                   jnp.concatenate([panel_pair[1], panel_pair[0]], axis=1)], axis=0)
        replica = lax.dot_general(mode_terms, stacked, (((1,), (1,)), ((), ())),
                                  preferred_element_type=jnp.float32).astype(jnp.bfloat16)
        widened = replica.astype(jnp.float32)
        energy = jnp.sum(widened * widened, axis=1) / receivers + 1e-6
        probing = jnp.concatenate([jnp.concatenate([snap_pair[0], snap_pair[1]], axis=1),
                                   jnp.concatenate([-snap_pair[1], snap_pair[0]], axis=1)], axis=0)
        projected = lax.dot_general(replica, probing, (((1,), (1,)), ((), ())), preferred_element_type=jnp.float32)
        received = jnp.sum(projected * projected, axis=1) / snap_count
        bartlett = (received / (2.0 * receivers * energy)).reshape(range_count, depth_count)
        return totals + bartlett, None

    start_totals = jnp.zeros((range_count, depth_count), jnp.float32)
    totals, _ = lax.scan(one_freq, start_totals, (shapes, panels, snapshots, wavenumbers, mode_counts, mode_mask))
    return totals


def reference(panels, snapshots, wavenumbers, mode_counts, mode_mask, mode_shapes):
    def one_range(row_index):
        return block_power(mode_shapes, 0, row_index, 1, panels, snapshots, wavenumbers, mode_counts, mode_mask)[0]

    surface = lax.map(one_range, jnp.arange(RANGES, dtype=jnp.int32))
    return surface / FREQS
```

```python
import functools

import jax
import jax.numpy as jnp
from jax import lax
from jax.experimental import pallas as pl
from jax.experimental.pallas import tpu as pltpu
from jax.sharding import PartitionSpec as P

MBLK = 128
ZBLK = 32
MESH = pl.DeviceIdType.MESH

range_anchor = 1000.0
range_step = 25.0


def surface_kernel(
    sizes,
    all_freqs,
    counts,
    mask,
    panels,
    snaps,
    cosines,
    sines,
    shapes,
    out,
    lhs_a,
    lhs_b,
    weights,
    energy,
    probe,
    power,
    rows_out,
    rows_in,
    energy_send,
    energy_recv,
    row_send,
    row_recv,
):
    groups, tiles, freqs = sizes
    freq_count, depth_count, modes = shapes.shape
    receivers = panels.shape[2]
    snap_count = snaps.shape[2]
    ranges = cosines.shape[1]
    own_ranges = ranges // groups
    chunk = receivers // own_ranges
    group = lax.axis_index("groups")
    tile = lax.axis_index("tile")
    freq = lax.axis_index("freq")
    peers = tiles * freqs
    me = tile * freqs + freq

    barrier = pltpu.get_barrier_semaphore()
    for step in range(1, peers):
        other = lax.rem(me + step, peers)
        pl.semaphore_signal(
            barrier,
            inc=1,
            device_id=(group, lax.div(other, freqs), lax.rem(other, freqs)),
            device_id_type=MESH,
        )
    for step in range(1, groups):
        pl.semaphore_signal(
            barrier,
            inc=1,
            device_id=(lax.rem(group + step, groups), tile, freq),
            device_id_type=MESH,
        )

    depth_blocks = depth_count // ZBLK
    mode_index = lax.broadcasted_iota(jnp.int32, (ZBLK, MBLK), 1)
    for f in range(freq_count):
        count = counts[f]
        for block in range(modes // MBLK):
            columns = pl.ds(block * MBLK, MBLK)
            inside = (mode_index + block * MBLK) < count
            parts = []
            for depth in range(depth_blocks):
                flag = mask[f, block, tile * depth_blocks + depth]
                live = jnp.where(inside, (flag == 1).astype(jnp.float32), 0.0)
                piece = shapes[f, pl.ds(depth * ZBLK, ZBLK), columns]
                parts.append(piece.astype(jnp.float32) * live)
            weights[f, columns, :] = jnp.concatenate(parts, axis=0).T.astype(jnp.bfloat16)

    first = group * own_ranges
    buffers = (lhs_a, lhs_b)

    def turn(f, buffer, j):
        rows = pl.ds(pl.multiple_of(j * chunk, chunk), chunk)
        imag_rows = pl.ds(pl.multiple_of(receivers + j * chunk, chunk), chunk)
        real = panels[f, 0, rows, :].astype(jnp.float32)
        imag = panels[f, 1, rows, :].astype(jnp.float32)
        for r in range(own_ranges):
            c = cosines[f, pl.ds(first + r, 1), :]
            s = sines[f, pl.ds(first + r, 1), :]
            buffer[r, rows, :] = (real * c - imag * s).astype(jnp.bfloat16)
            buffer[r, imag_rows, :] = (imag * c + real * s).astype(jnp.bfloat16)

    def measure_energy(f, buffer, j):
        replica = jnp.dot(buffer[j], weights[f], preferred_element_type=jnp.float32)
        total = jnp.sum(replica * replica, axis=0, keepdims=True)
        energy[group, f, pl.ds(j, 1), :] = total / receivers + 1e-6

    for f in range(freq_count + 1):

        def body(j, carry, f=f):
            if f < freq_count:
                turn(f, buffers[f % 2], j)
            if f > 0:
                measure_energy(f - 1, buffers[(f - 1) % 2], j)
            return carry

        lax.fori_loop(0, own_ranges, body, 0)

    pl.semaphore_wait(barrier, peers - 1 + groups - 1)
    energy_copies = []
    for step in range(1, groups):
        energy_copies.append(
            pltpu.make_async_remote_copy(
                src_ref=energy.at[group],
                dst_ref=energy.at[group],
                send_sem=energy_send.at[step],
                recv_sem=energy_recv.at[step],
                device_id=(lax.rem(group + step, groups), tile, freq),
                device_id_type=MESH,
            )
        )
    for copy in energy_copies:
        copy.start()

    for f in range(freq_count):
        pair = snaps[f].reshape(2 * snap_count, receivers)
        on_real = jnp.dot(pair, panels[f, 0], preferred_element_type=jnp.float32)
        on_imag = jnp.dot(pair, panels[f, 1], preferred_element_type=jnp.float32)
        real = on_real[:snap_count] + on_imag[snap_count:]
        imag = on_imag[:snap_count] - on_real[snap_count:]
        for r in range(ranges):
            c = cosines[f, pl.ds(r, 1), :]
            s = sines[f, pl.ds(r, 1), :]
            probe[r, pl.ds(0, snap_count), :] = (real * c - imag * s).astype(jnp.bfloat16)
            probe[r, pl.ds(snap_count, snap_count), :] = (imag * c + real * s).astype(jnp.bfloat16)
        step_ranges = own_ranges
        for start in range(0, ranges, step_ranges):
            left = probe[pl.ds(start, step_ranges)].reshape(step_ranges * 2 * snap_count, modes)
            projected = jnp.dot(left, weights[f], preferred_element_type=jnp.float32)
            squares = (projected * projected).reshape(step_ranges, 2 * snap_count, depth_count)
            power[f, pl.ds(start, step_ranges), :] = jnp.sum(squares, axis=1) / snap_count

    for copy in energy_copies:
        copy.wait()
    for g in range(groups):
        part = jnp.zeros((own_ranges, depth_count), jnp.float32)
        for f in range(freq_count):
            part += power[f, pl.ds(g * own_ranges, own_ranges), :] / (
                2.0 * receivers * energy[g, f]
            )
        for r in range(own_ranges):
            rows_out[g * own_ranges + r] = part[r : r + 1, :]

    row_copies = []
    for step in range(1, peers):
        other = lax.rem(me + step, peers)
        row_copies.append(
            pltpu.make_async_remote_copy(
                src_ref=rows_out.at[other],
                dst_ref=rows_in.at[me],
                send_sem=row_send.at[step],
                recv_sem=row_recv.at[step],
                device_id=(group, lax.div(other, freqs), lax.rem(other, freqs)),
                device_id_type=MESH,
            )
        )
    for copy in row_copies:
        copy.start()
    rows_in[me] = rows_out[me]
    for copy in row_copies:
        copy.wait()
    for t in range(tiles):
        total = rows_in[t * freqs]
        for f in range(1, freqs):
            total += rows_in[t * freqs + f]
        out[pl.ds(t, 1), :] = total / all_freqs


def on_device(panels, snapshots, wavenumbers, mode_counts, mode_mask, mode_shapes):
    groups, tiles, freqs = (lax.axis_size(name) for name in ("groups", "tile", "freq"))
    freq_count, depth_count, modes = mode_shapes.shape
    receivers = panels.shape[2]
    ranges = tiles * freqs
    own_ranges = ranges // groups
    snap_count = snapshots.shape[2]
    distances = range_anchor + range_step * jnp.arange(ranges, dtype=jnp.int32).astype(jnp.float32)
    phases = distances[None, :, None] * wavenumbers[:, None, :]
    vmem = pl.BlockSpec(memory_space=pltpu.VMEM)
    smem = pl.BlockSpec(memory_space=pltpu.SMEM)
    surface = pl.pallas_call(
        functools.partial(surface_kernel, (groups, tiles, freqs), freq_count * freqs),
        out_shape=jax.ShapeDtypeStruct((tiles, depth_count), jnp.float32),
        in_specs=[smem, smem] + [vmem] * 5,
        out_specs=vmem,
        scratch_shapes=[
            pltpu.VMEM((own_ranges, 2 * receivers, modes), jnp.bfloat16),
            pltpu.VMEM((own_ranges, 2 * receivers, modes), jnp.bfloat16),
            pltpu.VMEM((freq_count, modes, depth_count), jnp.bfloat16),
            pltpu.VMEM((groups, freq_count, own_ranges, depth_count), jnp.float32),
            pltpu.VMEM((ranges, 2 * snap_count, modes), jnp.bfloat16),
            pltpu.VMEM((freq_count, ranges, depth_count), jnp.float32),
            pltpu.VMEM((ranges, 1, depth_count), jnp.float32),
            pltpu.VMEM((ranges, 1, depth_count), jnp.float32),
            pltpu.SemaphoreType.DMA((groups,)),
            pltpu.SemaphoreType.DMA((groups,)),
            pltpu.SemaphoreType.DMA((ranges,)),
            pltpu.SemaphoreType.DMA((ranges,)),
        ],
        compiler_params=pltpu.CompilerParams(
            collective_id=0, has_side_effects=True, vmem_limit_bytes=48 * 1024 * 1024
        ),
    )(mode_counts, mode_mask, panels, snapshots, jnp.cos(phases), jnp.sin(phases), mode_shapes)
    return surface.reshape(1, tiles * depth_count)


def solution(mesh):
    in_specs = (
        P("freq", None, None, None),
        P(("groups", "freq"), None, None, None),
        P("freq", None),
        P("freq"),
        P("freq", None, None),
        P("freq", "tile", None),
    )
    out_specs = P(("groups", "tile", "freq"), None)
    return jax.shard_map(
        on_device, mesh=mesh, in_specs=in_specs, out_specs=out_specs, check_vma=False
    )
```

```python
import functools

import jax
import jax.numpy as jnp
from jax import lax
from jax.experimental import pallas as pl
from jax.experimental.pallas import tpu as pltpu
from jax.sharding import PartitionSpec as P

MBLK = 128
ZBLK = 32
MESH = pl.DeviceIdType.MESH

range_anchor = 1000.0
range_step = 25.0


def cosine_and_sine(angle):
    turns = jnp.floor(angle * 0.6366197723675814 + 0.5)
    rest = ((angle - turns * 1.5703125) - turns * 4.837512969970703125e-4) - (
        turns * 7.54978995489188216e-8
    )
    quarter = turns.astype(jnp.int32)
    square = rest * rest
    sine = rest + rest * square * (
        -1.6666654611e-1 + square * (8.3321608736e-3 - square * 1.9515295891e-4)
    )
    cosine = (1.0 - 0.5 * square) + square * square * (
        4.166664568298827e-2
        + square * (-1.388731625493765e-3 + square * 2.443315711809948e-5)
    )
    odd = (quarter & 1) == 1
    first = jnp.where(odd, sine, cosine)
    second = jnp.where(odd, cosine, sine)
    first = jnp.where(((quarter + 1) & 2) == 2, -first, first)
    second = jnp.where((quarter & 2) == 2, -second, second)
    return first, second


def surface_kernel(
    sizes,
    all_freqs,
    counts,
    mask_hbm,
    panels_hbm,
    snaps_hbm,
    wavenumbers_hbm,
    shapes_hbm,
    out,
    mask,
    panels,
    snaps,
    wavenumbers,
    shapes,
    cosines,
    sines,
    lhs_a,
    lhs_b,
    weights,
    energy,
    probe,
    panel_probe,
    power,
    rows_out,
    rows_in,
    table_sem,
    panel_sem,
    snap_sem,
    shape_sem,
    energy_send,
    energy_recv,
    row_send,
    row_recv,
):
    groups, tiles, freqs = sizes
    freq_count, depth_count, modes = shapes.shape
    receivers = panels.shape[2]
    snap_count = snaps.shape[2]
    ranges = cosines.shape[1]
    own_ranges = ranges // groups
    chunk = receivers // own_ranges
    group = lax.axis_index("groups")
    tile = lax.axis_index("tile")
    freq = lax.axis_index("freq")
    peers = tiles * freqs
    me = tile * freqs + freq

    number_copy = pltpu.make_async_copy(wavenumbers_hbm, wavenumbers, table_sem.at[0])
    number_copy.start()
    panel_copies, snap_copies, shape_copies = [], [], []
    for f in range(freq_count):
        panel_copies.append(
            pltpu.make_async_copy(panels_hbm.at[f], panels.at[f], panel_sem.at[f])
        )
        shape_copies.append(
            pltpu.make_async_copy(shapes_hbm.at[f], shapes.at[f], shape_sem.at[f])
        )
        snap_copies.append(pltpu.make_async_copy(snaps_hbm.at[f], snaps.at[f], snap_sem.at[f]))
    mask_copy = pltpu.make_async_copy(mask_hbm, mask, table_sem.at[1])
    panel_copies[0].start()
    mask_copy.start()
    for f in range(freq_count):
        shape_copies[f].start()
        snap_copies[f].start()
        if f + 1 < freq_count:
            panel_copies[f + 1].start()

    barrier = pltpu.get_barrier_semaphore()
    for step in range(1, peers):
        other = lax.rem(me + step, peers)
        pl.semaphore_signal(
            barrier,
            inc=1,
            device_id=(group, lax.div(other, freqs), lax.rem(other, freqs)),
            device_id_type=MESH,
        )
    for step in range(1, groups):
        pl.semaphore_signal(
            barrier,
            inc=1,
            device_id=(lax.rem(group + step, groups), tile, freq),
            device_id_type=MESH,
        )

    number_copy.wait()
    index = lax.broadcasted_iota(jnp.int32, (ranges, modes), 0)
    distance = range_anchor + range_step * index.astype(jnp.float32)
    for f in range(freq_count):
        c, s = cosine_and_sine(distance * wavenumbers[pl.ds(f, 1), :])
        cosines[f] = c
        sines[f] = s
    mask_copy.wait()

    block_count = mask.shape[2]
    depth_block = (
        lax.broadcasted_iota(jnp.int32, (block_count, depth_count), 1) + tile * depth_count
    ) // ZBLK
    one_hot = (
        depth_block == lax.broadcasted_iota(jnp.int32, (block_count, depth_count), 0)
    ).astype(jnp.bfloat16)
    mode_index = lax.broadcasted_iota(jnp.int32, (MBLK, depth_count), 0)

    def live_shapes(f):
        flags = mask[:, f, :].astype(jnp.float32).astype(jnp.bfloat16)
        live = jnp.dot(flags, one_hot, preferred_element_type=jnp.float32)
        for block in range(modes // MBLK):
            columns = pl.ds(block * MBLK, MBLK)
            inside = (mode_index + block * MBLK) < counts[f]
            keep = jnp.where(inside, live[block : block + 1, :], 0.0).astype(jnp.bfloat16)
            weights[f, columns, :] = shapes[f, :, columns].T * keep

    first = group * own_ranges
    buffers = (lhs_a, lhs_b)
    piece = 16

    def turn(f, buffer, j):
        for start in range(0, chunk, piece):
            base = j * chunk + start
            rows = pl.ds(pl.multiple_of(base, piece), piece)
            imag_rows = pl.ds(pl.multiple_of(receivers + base, piece), piece)
            real = panels[f, 0, rows, :].astype(jnp.float32)
            imag = panels[f, 1, rows, :].astype(jnp.float32)
            for r in range(own_ranges):
                c = cosines[f, pl.ds(first + r, 1), :]
                s = sines[f, pl.ds(first + r, 1), :]
                buffer[r, rows, :] = (real * c - imag * s).astype(jnp.bfloat16)
                buffer[r, imag_rows, :] = (imag * c + real * s).astype(jnp.bfloat16)

    def measure_energy(f, buffer, j):
        replica = jnp.dot(buffer[j], weights[f], preferred_element_type=jnp.float32)
        total = jnp.sum(replica * replica, axis=0, keepdims=True)
        energy[group, f, pl.ds(j, 1), :] = total / receivers + 1e-6

    def project_panels(f):
        pair = snaps[f].reshape(2 * snap_count, receivers)
        on_real = jnp.dot(pair, panels[f, 0], preferred_element_type=jnp.float32)
        on_imag = jnp.dot(pair, panels[f, 1], preferred_element_type=jnp.float32)
        panel_probe[0] = on_real[:snap_count] + on_imag[snap_count:]
        panel_probe[1] = on_imag[:snap_count] - on_real[snap_count:]

    def turn_probe(f, j):
        real, imag = panel_probe[0], panel_probe[1]
        for i in range(groups):
            r = j * groups + i
            c = cosines[f, pl.ds(r, 1), :]
            s = sines[f, pl.ds(r, 1), :]
            probe[f, r, pl.ds(0, snap_count), :] = (real * c - imag * s).astype(jnp.bfloat16)
            probe[f, r, pl.ds(snap_count, snap_count), :] = (imag * c + real * s).astype(
                jnp.bfloat16
            )

    for stage in range(freq_count + 1):
        if stage < freq_count:
            panel_copies[stage].wait()
        if stage > 0:
            shape_copies[stage - 1].wait()
            live_shapes(stage - 1)
            snap_copies[stage - 1].wait()
            project_panels(stage - 1)

        def body(j, carry, stage=stage):
            if stage < freq_count:
                turn(stage, buffers[stage % 2], j)
            if stage > 0:
                measure_energy(stage - 1, buffers[(stage - 1) % 2], j)
                turn_probe(stage - 1, j)
            return carry

        lax.fori_loop(0, own_ranges, body, 0)

    pl.semaphore_wait(barrier, peers - 1 + groups - 1)
    energy_copies = []
    for step in range(1, groups):
        energy_copies.append(
            pltpu.make_async_remote_copy(
                src_ref=energy.at[group],
                dst_ref=energy.at[group],
                send_sem=energy_send.at[step],
                recv_sem=energy_recv.at[step],
                device_id=(lax.rem(group + step, groups), tile, freq),
                device_id_type=MESH,
            )
        )
    for copy in energy_copies:
        copy.start()

    for f in range(freq_count):
        for start in range(0, ranges, own_ranges):
            left = probe[f, pl.ds(start, own_ranges)].reshape(-1, modes)
            projected = jnp.dot(left, weights[f], preferred_element_type=jnp.float32)
            squares = (projected * projected).reshape(own_ranges, 2 * snap_count, depth_count)
            power[f, pl.ds(start, own_ranges), :] = jnp.sum(squares, axis=1) / snap_count

    for copy in energy_copies:
        copy.wait()
    for g in range(groups):
        part = jnp.zeros((own_ranges, depth_count), jnp.float32)
        for f in range(freq_count):
            part += power[f, pl.ds(g * own_ranges, own_ranges), :] / (
                2.0 * receivers * energy[g, f]
            )
        for r in range(own_ranges):
            rows_out[g * own_ranges + r] = part[r : r + 1, :]

    row_copies = []
    for step in range(1, peers):
        other = lax.rem(me + step, peers)
        row_copies.append(
            pltpu.make_async_remote_copy(
                src_ref=rows_out.at[other],
                dst_ref=rows_in.at[me],
                send_sem=row_send.at[step],
                recv_sem=row_recv.at[step],
                device_id=(group, lax.div(other, freqs), lax.rem(other, freqs)),
                device_id_type=MESH,
            )
        )
    for copy in row_copies:
        copy.start()
    rows_in[me] = rows_out[me]
    for copy in row_copies:
        copy.wait()
    for t in range(tiles):
        total = rows_in[t * freqs]
        for f in range(1, freqs):
            total += rows_in[t * freqs + f]
        out[pl.ds(t, 1), :] = total / all_freqs


def on_device(panels, snapshots, wavenumbers, mode_counts, mode_mask, mode_shapes):
    groups, tiles, freqs = (lax.axis_size(name) for name in ("groups", "tile", "freq"))
    freq_count, depth_count, modes = mode_shapes.shape
    receivers = panels.shape[2]
    ranges = tiles * freqs
    own_ranges = ranges // groups
    snap_count = snapshots.shape[2]
    vmem = pl.BlockSpec(memory_space=pltpu.VMEM)
    smem = pl.BlockSpec(memory_space=pltpu.SMEM)
    hbm = pl.BlockSpec(memory_space=pltpu.HBM)
    by_block = jnp.swapaxes(mode_mask, 0, 1)
    inputs = (by_block, panels, snapshots, wavenumbers, mode_shapes)
    surface = pl.pallas_call(
        functools.partial(surface_kernel, (groups, tiles, freqs), freq_count * freqs),
        out_shape=jax.ShapeDtypeStruct((tiles, depth_count), jnp.float32),
        in_specs=[smem] + [hbm] * 5,
        out_specs=vmem,
        scratch_shapes=[pltpu.VMEM(value.shape, value.dtype) for value in inputs]
        + [
            pltpu.VMEM((freq_count, ranges, modes), jnp.float32),
            pltpu.VMEM((freq_count, ranges, modes), jnp.float32),
            pltpu.VMEM((own_ranges, 2 * receivers, modes), jnp.bfloat16),
            pltpu.VMEM((own_ranges, 2 * receivers, modes), jnp.bfloat16),
            pltpu.VMEM((freq_count, modes, depth_count), jnp.bfloat16),
            pltpu.VMEM((groups, freq_count, own_ranges, depth_count), jnp.float32),
            pltpu.VMEM((freq_count, ranges, 2 * snap_count, modes), jnp.bfloat16),
            pltpu.VMEM((2, snap_count, modes), jnp.float32),
            pltpu.VMEM((freq_count, ranges, depth_count), jnp.float32),
            pltpu.VMEM((ranges, 1, depth_count), jnp.float32),
            pltpu.VMEM((ranges, 1, depth_count), jnp.float32),
            pltpu.SemaphoreType.DMA((2,)),
            pltpu.SemaphoreType.DMA((freq_count,)),
            pltpu.SemaphoreType.DMA((freq_count,)),
            pltpu.SemaphoreType.DMA((freq_count,)),
            pltpu.SemaphoreType.DMA((groups,)),
            pltpu.SemaphoreType.DMA((groups,)),
            pltpu.SemaphoreType.DMA((ranges,)),
            pltpu.SemaphoreType.DMA((ranges,)),
        ],
        compiler_params=pltpu.CompilerParams(
            collective_id=0, has_side_effects=True, vmem_limit_bytes=56 * 1024 * 1024
        ),
    )(mode_counts, *inputs)
    return surface.reshape(1, tiles * depth_count)


def solution(mesh):
    in_specs = (
        P("freq", None, None, None),
        P(("groups", "freq"), None, None, None),
        P("freq", None),
        P("freq"),
        P("freq", None, None),
        P("freq", "tile", None),
    )
    out_specs = P(("groups", "tile", "freq"), None)
    return jax.shard_map(
        on_device, mesh=mesh, in_specs=in_specs, out_specs=out_specs, check_vma=False
    )
```

```python
import functools

import jax
import jax.numpy as jnp
from jax import lax
from jax.experimental import pallas as pl
from jax.experimental.pallas import tpu as pltpu
from jax.sharding import PartitionSpec as P

MBLK = 128
ZBLK = 32
MESH = pl.DeviceIdType.MESH

range_anchor = 1000.0
range_step = 25.0


def cosine_and_sine(angle):
    turns = jnp.floor(angle * 0.6366197723675814 + 0.5)
    rest = ((angle - turns * 1.5703125) - turns * 4.837512969970703125e-4) - (
        turns * 7.54978995489188216e-8
    )
    quarter = turns.astype(jnp.int32)
    square = rest * rest
    sine = rest + rest * square * (
        -1.6666654611e-1 + square * (8.3321608736e-3 - square * 1.9515295891e-4)
    )
    cosine = (1.0 - 0.5 * square) + square * square * (
        4.166664568298827e-2
        + square * (-1.388731625493765e-3 + square * 2.443315711809948e-5)
    )
    odd = (quarter & 1) == 1
    first = jnp.where(odd, sine, cosine)
    second = jnp.where(odd, cosine, sine)
    first = jnp.where(((quarter + 1) & 2) == 2, -first, first)
    second = jnp.where((quarter & 2) == 2, -second, second)
    return first, second


def surface_kernel(
    sizes,
    all_freqs,
    counts,
    mask_hbm,
    panels_hbm,
    snaps_hbm,
    wavenumbers_hbm,
    shapes_hbm,
    out,
    mask,
    panels,
    snaps,
    wavenumbers,
    shapes,
    cosines,
    sines,
    lhs_a,
    lhs_b,
    weights,
    energy,
    probe,
    panel_probe,
    power,
    rows_out,
    rows_in,
    table_sem,
    panel_sem,
    snap_sem,
    shape_sem,
    energy_send,
    energy_recv,
    row_send,
    row_recv,
):
    groups, tiles, freqs = sizes
    freq_count, depth_count, modes = shapes.shape
    receivers = panels.shape[2]
    snap_count = snaps.shape[2]
    ranges = cosines.shape[1]
    own_ranges = ranges // groups
    per = min(2, own_ranges)
    turns = own_ranges // per
    chunk = receivers // turns
    products = -(-2 * freq_count // turns)
    group = lax.axis_index("groups")
    tile = lax.axis_index("tile")
    freq = lax.axis_index("freq")
    peers = tiles * freqs
    me = tile * freqs + freq

    number_copy = pltpu.make_async_copy(wavenumbers_hbm, wavenumbers, table_sem.at[0])
    number_copy.start()
    panel_copies, snap_copies, shape_copies = [], [], []
    for f in range(freq_count):
        panel_copies.append(
            pltpu.make_async_copy(panels_hbm.at[f], panels.at[f], panel_sem.at[f])
        )
        shape_copies.append(
            pltpu.make_async_copy(shapes_hbm.at[f], shapes.at[f], shape_sem.at[f])
        )
        snap_copies.append(pltpu.make_async_copy(snaps_hbm.at[f], snaps.at[f], snap_sem.at[f]))
    mask_copy = pltpu.make_async_copy(mask_hbm, mask, table_sem.at[1])
    panel_copies[0].start()
    mask_copy.start()
    for f in range(freq_count):
        shape_copies[f].start()
        snap_copies[f].start()
        if f + 1 < freq_count:
            panel_copies[f + 1].start()

    barrier = pltpu.get_barrier_semaphore()
    for step in range(1, peers):
        other = lax.rem(me + step, peers)
        pl.semaphore_signal(
            barrier,
            inc=1,
            device_id=(group, lax.div(other, freqs), lax.rem(other, freqs)),
            device_id_type=MESH,
        )
    for step in range(1, groups):
        pl.semaphore_signal(
            barrier,
            inc=1,
            device_id=(lax.rem(group + step, groups), tile, freq),
            device_id_type=MESH,
        )

    number_copy.wait()
    index = lax.broadcasted_iota(jnp.int32, (ranges, modes), 0)
    distance = range_anchor + range_step * index.astype(jnp.float32)
    for f in range(freq_count):
        c, s = cosine_and_sine(distance * wavenumbers[pl.ds(f, 1), :])
        for r in range(ranges):
            cosines[f, r] = jnp.broadcast_to(c[r : r + 1, :], (8, modes))
            sines[f, r] = jnp.broadcast_to(s[r : r + 1, :], (8, modes))
    mask_copy.wait()

    block_count = mask.shape[2]
    depth_block = (
        lax.broadcasted_iota(jnp.int32, (block_count, depth_count), 1) + tile * depth_count
    ) // ZBLK
    one_hot = (
        depth_block == lax.broadcasted_iota(jnp.int32, (block_count, depth_count), 0)
    ).astype(jnp.bfloat16)
    mode_index = lax.broadcasted_iota(jnp.int32, (MBLK, depth_count), 0)

    def live_shapes(f):
        flags = mask[:, f, :].astype(jnp.float32).astype(jnp.bfloat16)
        live = jnp.dot(flags, one_hot, preferred_element_type=jnp.float32)
        for block in range(modes // MBLK):
            columns = pl.ds(block * MBLK, MBLK)
            inside = (mode_index + block * MBLK) < counts[f]
            keep = jnp.where(inside, live[block : block + 1, :], 0.0).astype(jnp.bfloat16)
            weights[f, columns, :] = shapes[f, :, columns].T * keep

    first = group * own_ranges
    buffers = (lhs_a, lhs_b)
    piece = 16

    def rotate(real, imag, f, r):
        c, s = cosines[f, r], sines[f, r]
        return (
            (real * c - imag * s).reshape(-1, modes).astype(jnp.bfloat16),
            (imag * c + real * s).reshape(-1, modes).astype(jnp.bfloat16),
        )

    def turn(f, buffer, j):
        for start in range(0, chunk, piece):
            base = j * chunk + start
            rows = pl.ds(pl.multiple_of(base, piece), piece)
            imag_rows = pl.ds(pl.multiple_of(receivers + base, piece), piece)
            real = panels[f, 0, rows, :].astype(jnp.float32).reshape(-1, 8, modes)
            imag = panels[f, 1, rows, :].astype(jnp.float32).reshape(-1, 8, modes)
            for r in range(own_ranges):
                buffer[r, rows, :], buffer[r, imag_rows, :] = rotate(real, imag, f, first + r)

    def measure_energy(f, buffer, j):
        left = buffer[pl.ds(j * per, per)].reshape(per * 2 * receivers, modes)
        replica = jnp.dot(left, weights[f], preferred_element_type=jnp.float32)
        squares = (replica * replica).reshape(per, 2 * receivers, depth_count)
        for i in range(per):
            total = jnp.sum(squares[i], axis=0, keepdims=True)
            energy[group, f, pl.ds(j * per + i, 1), :] = total / receivers + 1e-6

    def project_panels(j):
        for i in range(products):
            step = j * products + i
            f, half = lax.div(step, 2), lax.rem(step, 2)
            pair = snaps[f].reshape(2 * snap_count, receivers)
            panel_probe[f, half] = jnp.dot(
                pair, panels[f, half], preferred_element_type=jnp.float32
            )

    def turn_probe(f, j):
        on_real, on_imag = panel_probe[f, 0], panel_probe[f, 1]
        real = (on_real[:snap_count] + on_imag[snap_count:]).reshape(-1, 8, modes)
        imag = (on_imag[:snap_count] - on_real[snap_count:]).reshape(-1, 8, modes)
        for i in range(per * groups):
            r = j * per * groups + i
            top, bottom = rotate(real, imag, f, r)
            probe[f, r, pl.ds(0, snap_count), :] = top
            probe[f, r, pl.ds(snap_count, snap_count), :] = bottom

    for stage in range(freq_count + 1):
        if stage < min(2, freq_count):
            panel_copies[stage].wait()
        if stage > 0:
            shape_copies[stage - 1].wait()
            live_shapes(stage - 1)
        if stage == 1:
            for copy in panel_copies[2:] + snap_copies:
                copy.wait()
        if stage < 2:
            probes = []
        elif stage < freq_count:
            probes = [stage - 2]
        else:
            probes = list(range(freq_count - 2, freq_count))

        def body(j, carry, stage=stage, probes=probes):
            if stage > 0:
                measure_energy(stage - 1, buffers[(stage - 1) % 2], j)
            if stage < freq_count:
                turn(stage, buffers[stage % 2], j)
            if stage == 1:
                project_panels(j)
            for f in probes:
                turn_probe(f, j)
            return carry

        lax.fori_loop(0, turns, body, 0)

    pl.semaphore_wait(barrier, peers - 1 + groups - 1)
    energy_copies = []
    for step in range(1, groups):
        energy_copies.append(
            pltpu.make_async_remote_copy(
                src_ref=energy.at[group],
                dst_ref=energy.at[group],
                send_sem=energy_send.at[step],
                recv_sem=energy_recv.at[step],
                device_id=(lax.rem(group + step, groups), tile, freq),
                device_id_type=MESH,
            )
        )
    for copy in energy_copies:
        copy.start()

    for f in range(freq_count):
        for start in range(0, ranges, own_ranges):
            left = probe[f, pl.ds(start, own_ranges)].reshape(-1, modes)
            projected = jnp.dot(left, weights[f], preferred_element_type=jnp.float32)
            squares = (projected * projected).reshape(own_ranges, 2 * snap_count, depth_count)
            power[f, pl.ds(start, own_ranges), :] = jnp.sum(squares, axis=1) / snap_count

    for copy in energy_copies:
        copy.wait()
    for g in range(groups):
        part = jnp.zeros((own_ranges, depth_count), jnp.float32)
        for f in range(freq_count):
            part += power[f, pl.ds(g * own_ranges, own_ranges), :] / (
                2.0 * receivers * energy[g, f]
            )
        for r in range(own_ranges):
            rows_out[g * own_ranges + r] = part[r : r + 1, :]

    row_copies = []
    for step in range(1, peers):
        other = lax.rem(me + step, peers)
        row_copies.append(
            pltpu.make_async_remote_copy(
                src_ref=rows_out.at[other],
                dst_ref=rows_in.at[me],
                send_sem=row_send.at[step],
                recv_sem=row_recv.at[step],
                device_id=(group, lax.div(other, freqs), lax.rem(other, freqs)),
                device_id_type=MESH,
            )
        )
    for copy in row_copies:
        copy.start()
    rows_in[me] = rows_out[me]
    for copy in row_copies:
        copy.wait()
    for t in range(tiles):
        total = rows_in[t * freqs]
        for f in range(1, freqs):
            total += rows_in[t * freqs + f]
        out[t] = total / all_freqs


def on_device(panels, snapshots, wavenumbers, mode_counts, mode_mask, mode_shapes):
    groups, tiles, freqs = (lax.axis_size(name) for name in ("groups", "tile", "freq"))
    freq_count, depth_count, modes = mode_shapes.shape
    receivers = panels.shape[2]
    ranges = tiles * freqs
    own_ranges = ranges // groups
    snap_count = snapshots.shape[2]
    vmem = pl.BlockSpec(memory_space=pltpu.VMEM)
    smem = pl.BlockSpec(memory_space=pltpu.SMEM)
    hbm = pl.BlockSpec(memory_space=pltpu.HBM)
    by_block = jnp.swapaxes(mode_mask, 0, 1)
    inputs = (by_block, panels, snapshots, wavenumbers, mode_shapes)
    surface = pl.pallas_call(
        functools.partial(surface_kernel, (groups, tiles, freqs), freq_count * freqs),
        out_shape=jax.ShapeDtypeStruct((tiles, 1, depth_count), jnp.float32),
        in_specs=[smem] + [hbm] * 5,
        out_specs=vmem,
        scratch_shapes=[pltpu.VMEM(value.shape, value.dtype) for value in inputs]
        + [
            pltpu.VMEM((freq_count, ranges, 8, modes), jnp.float32),
            pltpu.VMEM((freq_count, ranges, 8, modes), jnp.float32),
            pltpu.VMEM((own_ranges, 2 * receivers, modes), jnp.bfloat16),
            pltpu.VMEM((own_ranges, 2 * receivers, modes), jnp.bfloat16),
            pltpu.VMEM((freq_count, modes, depth_count), jnp.bfloat16),
            pltpu.VMEM((groups, freq_count, own_ranges, depth_count), jnp.float32),
            pltpu.VMEM((freq_count, ranges, 2 * snap_count, modes), jnp.bfloat16),
            pltpu.VMEM((freq_count, 2, 2 * snap_count, modes), jnp.float32),
            pltpu.VMEM((freq_count, ranges, depth_count), jnp.float32),
            pltpu.VMEM((ranges, 1, depth_count), jnp.float32),
            pltpu.VMEM((ranges, 1, depth_count), jnp.float32),
            pltpu.SemaphoreType.DMA((2,)),
            pltpu.SemaphoreType.DMA((freq_count,)),
            pltpu.SemaphoreType.DMA((freq_count,)),
            pltpu.SemaphoreType.DMA((freq_count,)),
            pltpu.SemaphoreType.DMA((groups,)),
            pltpu.SemaphoreType.DMA((groups,)),
            pltpu.SemaphoreType.DMA((ranges,)),
            pltpu.SemaphoreType.DMA((ranges,)),
        ],
        compiler_params=pltpu.CompilerParams(
            collective_id=0, has_side_effects=True, vmem_limit_bytes=56 * 1024 * 1024
        ),
    )(mode_counts, *inputs)
    return surface.reshape(1, tiles * depth_count)


def solution(mesh):
    in_specs = (
        P("freq", None, None, None),
        P(("groups", "freq"), None, None, None),
        P("freq", None),
        P("freq"),
        P("freq", None, None),
        P("freq", "tile", None),
    )
    out_specs = P(("groups", "tile", "freq"), None)
    return jax.shard_map(
        on_device, mesh=mesh, in_specs=in_specs, out_specs=out_specs, check_vma=False
    )
```

```python
import functools

import jax
import jax.numpy as jnp
from jax import lax
from jax.experimental import pallas as pl
from jax.experimental.pallas import tpu as pltpu
from jax.sharding import PartitionSpec as P

MBLK = 128
ZBLK = 32
MESH = pl.DeviceIdType.MESH

range_anchor = 1000.0
range_step = 25.0


def cosine_and_sine(angle):
    turns = jnp.floor(angle * 0.6366197723675814 + 0.5)
    rest = ((angle - turns * 1.5703125) - turns * 4.837512969970703125e-4) - (
        turns * 7.54978995489188216e-8
    )
    quarter = turns.astype(jnp.int32)
    square = rest * rest
    sine = rest + rest * square * (
        -1.6666654611e-1 + square * (8.3321608736e-3 - square * 1.9515295891e-4)
    )
    cosine = (1.0 - 0.5 * square) + square * square * (
        4.166664568298827e-2
        + square * (-1.388731625493765e-3 + square * 2.443315711809948e-5)
    )
    odd = (quarter & 1) == 1
    first = jnp.where(odd, sine, cosine)
    second = jnp.where(odd, cosine, sine)
    first = jnp.where(((quarter + 1) & 2) == 2, -first, first)
    second = jnp.where((quarter & 2) == 2, -second, second)
    return first, second


def surface_kernel(
    sizes,
    all_freqs,
    counts,
    mask_hbm,
    panels_hbm,
    snaps_hbm,
    wavenumbers_hbm,
    shapes_hbm,
    out,
    mask,
    panels,
    snaps,
    wavenumbers,
    shapes,
    cosines,
    sines,
    lhs_a,
    lhs_b,
    weights,
    energy,
    probe,
    panel_probe,
    power,
    rows_out,
    rows_in,
    table_sem,
    panel_sem,
    snap_sem,
    shape_sem,
    energy_send,
    energy_recv,
    row_send,
    row_recv,
):
    groups, tiles, freqs = sizes
    freq_count, depth_count, modes = shapes.shape
    receivers = panels.shape[2]
    snap_count = snaps.shape[2]
    ranges = cosines.shape[1]
    own_ranges = ranges // groups
    per = min(4, own_ranges)
    turns = own_ranges // per
    chunk = receivers // turns
    group = lax.axis_index("groups")
    tile = lax.axis_index("tile")
    freq = lax.axis_index("freq")
    peers = tiles * freqs
    me = tile * freqs + freq

    number_copy = pltpu.make_async_copy(wavenumbers_hbm, wavenumbers, table_sem.at[0])
    number_copy.start()
    panel_copies, snap_copies, shape_copies = [], [], []
    for f in range(freq_count):
        panel_copies.append(
            pltpu.make_async_copy(panels_hbm.at[f], panels.at[f], panel_sem.at[f])
        )
        shape_copies.append(
            pltpu.make_async_copy(shapes_hbm.at[f], shapes.at[f], shape_sem.at[f])
        )
        snap_copies.append(pltpu.make_async_copy(snaps_hbm.at[f], snaps.at[f], snap_sem.at[f]))
    mask_copy = pltpu.make_async_copy(mask_hbm, mask, table_sem.at[1])
    panel_copies[0].start()
    mask_copy.start()
    for f in range(freq_count):
        shape_copies[f].start()
        snap_copies[f].start()
        if f + 1 < freq_count:
            panel_copies[f + 1].start()

    barrier = pltpu.get_barrier_semaphore()
    for step in range(1, peers):
        other = lax.rem(me + step, peers)
        pl.semaphore_signal(
            barrier,
            inc=1,
            device_id=(group, lax.div(other, freqs), lax.rem(other, freqs)),
            device_id_type=MESH,
        )
    for step in range(1, groups):
        pl.semaphore_signal(
            barrier,
            inc=1,
            device_id=(lax.rem(group + step, groups), tile, freq),
            device_id_type=MESH,
        )

    number_copy.wait()
    index = lax.broadcasted_iota(jnp.int32, (ranges, modes), 0)
    distance = range_anchor + range_step * index.astype(jnp.float32)
    for f in range(freq_count):
        c, s = cosine_and_sine(distance * wavenumbers[pl.ds(f, 1), :])
        for r in range(ranges):
            cosines[f, r] = jnp.broadcast_to(c[r : r + 1, :], (8, modes))
            sines[f, r] = jnp.broadcast_to(s[r : r + 1, :], (8, modes))
    mask_copy.wait()

    block_count = mask.shape[2]
    depth_block = (
        lax.broadcasted_iota(jnp.int32, (block_count, depth_count), 1) + tile * depth_count
    ) // ZBLK
    one_hot = (
        depth_block == lax.broadcasted_iota(jnp.int32, (block_count, depth_count), 0)
    ).astype(jnp.bfloat16)
    mode_index = lax.broadcasted_iota(jnp.int32, (MBLK, depth_count), 0)

    def live_shapes(f):
        flags = mask[:, f, :].astype(jnp.float32).astype(jnp.bfloat16)
        live = jnp.dot(flags, one_hot, preferred_element_type=jnp.float32)
        for block in range(modes // MBLK):
            columns = pl.ds(block * MBLK, MBLK)
            inside = (mode_index + block * MBLK) < counts[f]
            keep = jnp.where(inside, live[block : block + 1, :], 0.0).astype(jnp.bfloat16)
            weights[f, columns, :] = shapes[f, :, columns].T * keep

    first = group * own_ranges
    buffers = (lhs_a, lhs_b)
    piece = 16

    def rotate(real, imag, f, r):
        c, s = cosines[f, r], sines[f, r]
        return (
            (real * c - imag * s).reshape(-1, modes).astype(jnp.bfloat16),
            (imag * c + real * s).reshape(-1, modes).astype(jnp.bfloat16),
        )

    def turn(f, buffer, lowest, count):
        for start in range(0, count, piece):
            base = lowest + start
            rows = pl.ds(pl.multiple_of(base, piece), piece)
            imag_rows = pl.ds(pl.multiple_of(receivers + base, piece), piece)
            real = panels[f, 0, rows, :].astype(jnp.float32).reshape(-1, 8, modes)
            imag = panels[f, 1, rows, :].astype(jnp.float32).reshape(-1, 8, modes)
            for r in range(own_ranges):
                buffer[r, rows, :], buffer[r, imag_rows, :] = rotate(real, imag, f, first + r)

    def measure_energy(f, buffer, j):
        left = buffer[pl.ds(j * per, per)].reshape(per * 2 * receivers, modes)
        replica = jnp.dot(left, weights[f], preferred_element_type=jnp.float32)
        squares = (replica * replica).reshape(per, 2 * receivers, depth_count)
        for i in range(per):
            total = jnp.sum(squares[i], axis=0, keepdims=True)
            energy[group, f, pl.ds(j * per + i, 1), :] = total / receivers + 1e-6

    def project_panels(f):
        pair = snaps[f].reshape(2 * snap_count, receivers)
        for half in range(2):
            panel_probe[f, half] = jnp.dot(
                pair, panels[f, half], preferred_element_type=jnp.float32
            )

    def turn_probe(f, j):
        on_real, on_imag = panel_probe[f, 0], panel_probe[f, 1]
        real = (on_real[:snap_count] + on_imag[snap_count:]).reshape(-1, 8, modes)
        imag = (on_imag[:snap_count] - on_real[snap_count:]).reshape(-1, 8, modes)
        for i in range(per * groups):
            r = j * per * groups + i
            top, bottom = rotate(real, imag, f, r)
            probe[f, r, pl.ds(0, snap_count), :] = top
            probe[f, r, pl.ds(snap_count, snap_count), :] = bottom

    part_rows = receivers // freq_count
    for f in range(freq_count):
        panel_copies[f].wait()
        shape_copies[f].wait()
        snap_copies[f].wait()
        live_shapes(f)
        project_panels(f)
        turn(0, buffers[0], f * part_rows, part_rows)

    for stage in range(1, freq_count + 1):

        def body(j, carry, stage=stage):
            measure_energy(stage - 1, buffers[(stage - 1) % 2], j)
            if stage < freq_count:
                turn(stage, buffers[stage % 2], j * chunk, chunk)
            turn_probe(stage - 1, j)
            return carry

        lax.fori_loop(0, turns, body, 0)

    pl.semaphore_wait(barrier, peers - 1 + groups - 1)
    energy_copies = []
    for step in range(1, groups):
        energy_copies.append(
            pltpu.make_async_remote_copy(
                src_ref=energy.at[group],
                dst_ref=energy.at[group],
                send_sem=energy_send.at[step],
                recv_sem=energy_recv.at[step],
                device_id=(lax.rem(group + step, groups), tile, freq),
                device_id_type=MESH,
            )
        )
    for copy in energy_copies:
        copy.start()

    for f in range(freq_count):
        left = probe[f].reshape(-1, modes)
        projected = jnp.dot(left, weights[f], preferred_element_type=jnp.float32)
        squares = (projected * projected).reshape(ranges, 2 * snap_count, depth_count)
        power[f] = jnp.sum(squares, axis=1) / snap_count

    for copy in energy_copies:
        copy.wait()
    for g in range(groups):
        part = jnp.zeros((own_ranges, depth_count), jnp.float32)
        for f in range(freq_count):
            part += power[f, pl.ds(g * own_ranges, own_ranges), :] / (
                2.0 * receivers * energy[g, f]
            )
        for r in range(own_ranges):
            rows_out[g * own_ranges + r] = part[r : r + 1, :]

    row_copies = []
    for step in range(1, peers):
        other = lax.rem(me + step, peers)
        row_copies.append(
            pltpu.make_async_remote_copy(
                src_ref=rows_out.at[other],
                dst_ref=rows_in.at[me],
                send_sem=row_send.at[step],
                recv_sem=row_recv.at[step],
                device_id=(group, lax.div(other, freqs), lax.rem(other, freqs)),
                device_id_type=MESH,
            )
        )
    for copy in row_copies:
        copy.start()
    rows_in[me] = rows_out[me]
    for copy in row_copies:
        copy.wait()
    for t in range(tiles):
        total = rows_in[t * freqs]
        for f in range(1, freqs):
            total += rows_in[t * freqs + f]
        out[t] = total / all_freqs


def on_device(panels, snapshots, wavenumbers, mode_counts, mode_mask, mode_shapes):
    groups, tiles, freqs = (lax.axis_size(name) for name in ("groups", "tile", "freq"))
    freq_count, depth_count, modes = mode_shapes.shape
    receivers = panels.shape[2]
    ranges = tiles * freqs
    own_ranges = ranges // groups
    snap_count = snapshots.shape[2]
    vmem = pl.BlockSpec(memory_space=pltpu.VMEM)
    smem = pl.BlockSpec(memory_space=pltpu.SMEM)
    hbm = pl.BlockSpec(memory_space=pltpu.HBM)
    by_block = jnp.swapaxes(mode_mask, 0, 1)
    inputs = (by_block, panels, snapshots, wavenumbers, mode_shapes)
    surface = pl.pallas_call(
        functools.partial(surface_kernel, (groups, tiles, freqs), freq_count * freqs),
        out_shape=jax.ShapeDtypeStruct((tiles, 1, depth_count), jnp.float32),
        in_specs=[smem] + [hbm] * 5,
        out_specs=vmem,
        scratch_shapes=[pltpu.VMEM(value.shape, value.dtype) for value in inputs]
        + [
            pltpu.VMEM((freq_count, ranges, 8, modes), jnp.float32),
            pltpu.VMEM((freq_count, ranges, 8, modes), jnp.float32),
            pltpu.VMEM((own_ranges, 2 * receivers, modes), jnp.bfloat16),
            pltpu.VMEM((own_ranges, 2 * receivers, modes), jnp.bfloat16),
            pltpu.VMEM((freq_count, modes, depth_count), jnp.bfloat16),
            pltpu.VMEM((groups, freq_count, own_ranges, depth_count), jnp.float32),
            pltpu.VMEM((freq_count, ranges, 2 * snap_count, modes), jnp.bfloat16),
            pltpu.VMEM((freq_count, 2, 2 * snap_count, modes), jnp.float32),
            pltpu.VMEM((freq_count, ranges, depth_count), jnp.float32),
            pltpu.VMEM((ranges, 1, depth_count), jnp.float32),
            pltpu.VMEM((ranges, 1, depth_count), jnp.float32),
            pltpu.SemaphoreType.DMA((2,)),
            pltpu.SemaphoreType.DMA((freq_count,)),
            pltpu.SemaphoreType.DMA((freq_count,)),
            pltpu.SemaphoreType.DMA((freq_count,)),
            pltpu.SemaphoreType.DMA((groups,)),
            pltpu.SemaphoreType.DMA((groups,)),
            pltpu.SemaphoreType.DMA((ranges,)),
            pltpu.SemaphoreType.DMA((ranges,)),
        ],
        compiler_params=pltpu.CompilerParams(
            collective_id=0, has_side_effects=True, vmem_limit_bytes=56 * 1024 * 1024
        ),
    )(mode_counts, *inputs)
    return surface.reshape(1, tiles * depth_count)


def solution(mesh):
    in_specs = (
        P("freq", None, None, None),
        P(("groups", "freq"), None, None, None),
        P("freq", None),
        P("freq"),
        P("freq", None, None),
        P("freq", "tile", None),
    )
    out_specs = P(("groups", "tile", "freq"), None)
    return jax.shard_map(
        on_device, mesh=mesh, in_specs=in_specs, out_specs=out_specs, check_vma=False
    )
```

```python
import functools

import jax
import jax.numpy as jnp
from jax import lax
from jax.experimental import pallas as pl
from jax.experimental.pallas import tpu as pltpu
from jax.sharding import PartitionSpec as P

MBLK = 128
ZBLK = 32
MESH = pl.DeviceIdType.MESH

range_anchor = 1000.0
range_step = 25.0


def cosine_and_sine(angle):
    turns = jnp.floor(angle * 0.6366197723675814 + 0.5)
    rest = ((angle - turns * 1.5703125) - turns * 4.837512969970703125e-4) - (
        turns * 7.54978995489188216e-8
    )
    quarter = turns.astype(jnp.int32)
    square = rest * rest
    sine = rest + rest * square * (
        -1.6666654611e-1 + square * (8.3321608736e-3 - square * 1.9515295891e-4)
    )
    cosine = (1.0 - 0.5 * square) + square * square * (
        4.166664568298827e-2
        + square * (-1.388731625493765e-3 + square * 2.443315711809948e-5)
    )
    odd = (quarter & 1) == 1
    first = jnp.where(odd, sine, cosine)
    second = jnp.where(odd, cosine, sine)
    first = jnp.where(((quarter + 1) & 2) == 2, -first, first)
    second = jnp.where((quarter & 2) == 2, -second, second)
    return first, second


def surface_kernel(
    sizes,
    all_freqs,
    counts,
    mask_hbm,
    panels_hbm,
    snaps_hbm,
    wavenumbers_hbm,
    shapes_hbm,
    out,
    mask,
    panels,
    snaps,
    wavenumbers,
    shapes,
    cosines,
    sines,
    lhs_a,
    lhs_b,
    weights,
    energy,
    probe,
    panel_probe,
    power,
    rows_out,
    rows_in,
    table_sem,
    panel_sem,
    snap_sem,
    shape_sem,
    energy_send,
    energy_recv,
    row_send,
    row_recv,
):
    groups, tiles, freqs = sizes
    freq_count, depth_count, modes = shapes.shape
    receivers = panels.shape[2]
    snap_count = snaps.shape[2]
    ranges = rows_in.shape[0]
    table_rows = cosines.shape[1]
    own_ranges = ranges // groups
    per = min(2, own_ranges // 2)
    turns = own_ranges // 2 // per
    chunk = receivers // turns
    group = lax.axis_index("groups")
    tile = lax.axis_index("tile")
    freq = lax.axis_index("freq")
    peers = tiles * freqs
    me = tile * freqs + freq

    number_copy = pltpu.make_async_copy(wavenumbers_hbm, wavenumbers, table_sem.at[0])
    number_copy.start()
    panel_copies, snap_copies, shape_copies = [], [], []
    for f in range(freq_count):
        panel_copies.append(
            pltpu.make_async_copy(panels_hbm.at[f], panels.at[f], panel_sem.at[f])
        )
        shape_copies.append(
            pltpu.make_async_copy(shapes_hbm.at[f], shapes.at[f], shape_sem.at[f])
        )
        snap_copies.append(pltpu.make_async_copy(snaps_hbm.at[f], snaps.at[f], snap_sem.at[f]))
    mask_copy = pltpu.make_async_copy(mask_hbm, mask, table_sem.at[1])
    panel_copies[0].start()
    mask_copy.start()
    for f in range(freq_count):
        shape_copies[f].start()
        snap_copies[f].start()
        if f + 1 < freq_count:
            panel_copies[f + 1].start()

    barrier = pltpu.get_barrier_semaphore()
    for step in range(1, peers):
        other = lax.rem(me + step, peers)
        pl.semaphore_signal(
            barrier,
            inc=1,
            device_id=(group, lax.div(other, freqs), lax.rem(other, freqs)),
            device_id_type=MESH,
        )
    for step in range(1, groups):
        pl.semaphore_signal(
            barrier,
            inc=1,
            device_id=(lax.rem(group + step, groups), tile, freq),
            device_id_type=MESH,
        )

    number_copy.wait()
    pairs, all_pairs = own_ranges // 2, ranges // 2
    index = lax.broadcasted_iota(jnp.int32, (table_rows, modes), 0)
    away = range_step * (index.astype(jnp.float32) + 0.5)
    own_first = (group * own_ranges).astype(jnp.float32)
    own_middle = range_anchor + range_step * (own_first + 0.5 * (own_ranges - 1))
    all_middle = range_anchor + range_step * (0.5 * (ranges - 1))
    middle = jnp.where(index == all_pairs, own_middle, all_middle)
    distance = jnp.where(index < all_pairs, away, middle)
    for f in range(freq_count):
        c, s = cosine_and_sine(distance * wavenumbers[pl.ds(f, 1), :])
        for r in range(table_rows):
            cosines[f, r] = jnp.broadcast_to(c[r : r + 1, :], (8, modes))
            sines[f, r] = jnp.broadcast_to(s[r : r + 1, :], (8, modes))
    mask_copy.wait()

    block_count = mask.shape[2]
    depth_block = (
        lax.broadcasted_iota(jnp.int32, (block_count, depth_count), 1) + tile * depth_count
    ) // ZBLK
    one_hot = (
        depth_block == lax.broadcasted_iota(jnp.int32, (block_count, depth_count), 0)
    ).astype(jnp.bfloat16)
    mode_index = lax.broadcasted_iota(jnp.int32, (MBLK, depth_count), 0)

    def live_shapes(f):
        flags = mask[:, f, :].astype(jnp.float32).astype(jnp.bfloat16)
        live = jnp.dot(flags, one_hot, preferred_element_type=jnp.float32)
        for block in range(modes // MBLK):
            columns = pl.ds(block * MBLK, MBLK)
            inside = (mode_index + block * MBLK) < counts[f]
            keep = jnp.where(inside, live[block : block + 1, :], 0.0).astype(jnp.bfloat16)
            weights[f, columns, :] = shapes[f, :, columns].T * keep

    buffers = (lhs_a, lhs_b)
    piece = 16

    def rotate(real, imag, f, row):
        c, s = cosines[f, row], sines[f, row]
        return real * c - imag * s, imag * c + real * s

    def scale(value, table):
        return (value * table).reshape(-1, modes).astype(jnp.bfloat16)

    def turn(f, buffer, lowest, count):
        for start in range(0, count, piece):
            base = lowest + start
            rows = [
                pl.ds(pl.multiple_of(part * receivers + base, piece), piece) for part in range(4)
            ]
            real = panels[f, 0, rows[0], :].astype(jnp.float32).reshape(-1, 8, modes)
            imag = panels[f, 1, rows[0], :].astype(jnp.float32).reshape(-1, 8, modes)
            real, imag = rotate(real, imag, f, all_pairs)
            for i in range(pairs):
                c, s = cosines[f, i], sines[f, i]
                buffer[i, rows[0], :] = scale(real, c)
                buffer[i, rows[1], :] = scale(imag, c)
                buffer[i, rows[2], :] = scale(real, s)
                buffer[i, rows[3], :] = scale(imag, s)

    def two_sides(product, count):
        even_real, even_imag = product[:count], product[count : 2 * count]
        odd_real, odd_imag = product[2 * count : 3 * count], product[3 * count :]
        beyond_real, beyond_imag = even_real - odd_imag, even_imag + odd_real
        before_real, before_imag = even_real + odd_imag, even_imag - odd_real
        beyond = beyond_real * beyond_real + beyond_imag * beyond_imag
        before = before_real * before_real + before_imag * before_imag
        return jnp.sum(beyond, axis=0, keepdims=True), jnp.sum(before, axis=0, keepdims=True)

    def measure_energy(f, buffer, j):
        left = buffer[pl.ds(j * per, per)].reshape(per * 4 * receivers, modes)
        product = jnp.dot(left, weights[f], preferred_element_type=jnp.float32)
        for i in range(per):
            lowest = i * 4 * receivers
            beyond, before = two_sides(product[lowest : lowest + 4 * receivers], receivers)
            step = j * per + i
            energy[group, f, pl.ds(pairs + step, 1), :] = beyond / receivers + 1e-6
            energy[group, f, pl.ds(pairs - 1 - step, 1), :] = before / receivers + 1e-6

    def project_panels(f):
        pair = snaps[f].reshape(2 * snap_count, receivers)
        for half in range(2):
            panel_probe[f, half] = jnp.dot(
                pair, panels[f, half], preferred_element_type=jnp.float32
            )

    def turn_probe(f, j):
        on_real, on_imag = panel_probe[f, 0], panel_probe[f, 1]
        real = (on_real[:snap_count] + on_imag[snap_count:]).reshape(-1, 8, modes)
        imag = (on_imag[:snap_count] - on_real[snap_count:]).reshape(-1, 8, modes)
        real, imag = rotate(real, imag, f, all_pairs + 1)
        for i in range(per * groups):
            step = j * per * groups + i
            c, s = cosines[f, step], sines[f, step]
            probe[f, step, pl.ds(0, snap_count), :] = scale(real, c)
            probe[f, step, pl.ds(snap_count, snap_count), :] = scale(imag, c)
            probe[f, step, pl.ds(2 * snap_count, snap_count), :] = scale(real, s)
            probe[f, step, pl.ds(3 * snap_count, snap_count), :] = scale(imag, s)

    part_rows = receivers // freq_count
    for f in range(freq_count):
        panel_copies[f].wait()
        shape_copies[f].wait()
        snap_copies[f].wait()
        live_shapes(f)
        project_panels(f)
        turn(0, buffers[0], f * part_rows, part_rows)

    for stage in range(1, freq_count + 1):

        def body(j, carry, stage=stage):
            measure_energy(stage - 1, buffers[(stage - 1) % 2], j)
            if stage < freq_count:
                turn(stage, buffers[stage % 2], j * chunk, chunk)
            turn_probe(stage - 1, j)
            return carry

        lax.fori_loop(0, turns, body, 0)

    pl.semaphore_wait(barrier, peers - 1 + groups - 1)
    energy_copies = []
    for step in range(1, groups):
        energy_copies.append(
            pltpu.make_async_remote_copy(
                src_ref=energy.at[group],
                dst_ref=energy.at[group],
                send_sem=energy_send.at[step],
                recv_sem=energy_recv.at[step],
                device_id=(lax.rem(group + step, groups), tile, freq),
                device_id_type=MESH,
            )
        )
    for copy in energy_copies:
        copy.start()

    for f in range(freq_count):
        left = probe[f].reshape(-1, modes)
        projected = jnp.dot(left, weights[f], preferred_element_type=jnp.float32)
        for i in range(all_pairs):
            lowest = i * 4 * snap_count
            beyond, before = two_sides(projected[lowest : lowest + 4 * snap_count], snap_count)
            power[f, pl.ds(all_pairs + i, 1), :] = beyond / snap_count
            power[f, pl.ds(all_pairs - 1 - i, 1), :] = before / snap_count

    for copy in energy_copies:
        copy.wait()
    for g in range(groups):
        part = jnp.zeros((own_ranges, depth_count), jnp.float32)
        for f in range(freq_count):
            part += power[f, pl.ds(g * own_ranges, own_ranges), :] / (
                2.0 * receivers * energy[g, f]
            )
        for r in range(own_ranges):
            rows_out[g * own_ranges + r] = part[r : r + 1, :]

    row_copies = []
    for step in range(1, peers):
        other = lax.rem(me + step, peers)
        row_copies.append(
            pltpu.make_async_remote_copy(
                src_ref=rows_out.at[other],
                dst_ref=rows_in.at[me],
                send_sem=row_send.at[step],
                recv_sem=row_recv.at[step],
                device_id=(group, lax.div(other, freqs), lax.rem(other, freqs)),
                device_id_type=MESH,
            )
        )
    for copy in row_copies:
        copy.start()
    rows_in[me] = rows_out[me]
    for copy in row_copies:
        copy.wait()
    for t in range(tiles):
        total = rows_in[t * freqs]
        for f in range(1, freqs):
            total += rows_in[t * freqs + f]
        out[t] = total / all_freqs


def on_device(panels, snapshots, wavenumbers, mode_counts, mode_mask, mode_shapes):
    groups, tiles, freqs = (lax.axis_size(name) for name in ("groups", "tile", "freq"))
    freq_count, depth_count, modes = mode_shapes.shape
    receivers = panels.shape[2]
    ranges = tiles * freqs
    own_ranges = ranges // groups
    snap_count = snapshots.shape[2]
    vmem = pl.BlockSpec(memory_space=pltpu.VMEM)
    smem = pl.BlockSpec(memory_space=pltpu.SMEM)
    hbm = pl.BlockSpec(memory_space=pltpu.HBM)
    by_block = jnp.swapaxes(mode_mask, 0, 1)
    inputs = (by_block, panels, snapshots, wavenumbers, mode_shapes)
    surface = pl.pallas_call(
        functools.partial(surface_kernel, (groups, tiles, freqs), freq_count * freqs),
        out_shape=jax.ShapeDtypeStruct((tiles, 1, depth_count), jnp.float32),
        in_specs=[smem] + [hbm] * 5,
        out_specs=vmem,
        scratch_shapes=[pltpu.VMEM(value.shape, value.dtype) for value in inputs]
        + [
            pltpu.VMEM((freq_count, ranges // 2 + 2, 8, modes), jnp.float32),
            pltpu.VMEM((freq_count, ranges // 2 + 2, 8, modes), jnp.float32),
            pltpu.VMEM((own_ranges // 2, 4 * receivers, modes), jnp.bfloat16),
            pltpu.VMEM((own_ranges // 2, 4 * receivers, modes), jnp.bfloat16),
            pltpu.VMEM((freq_count, modes, depth_count), jnp.bfloat16),
            pltpu.VMEM((groups, freq_count, own_ranges, depth_count), jnp.float32),
            pltpu.VMEM((freq_count, ranges // 2, 4 * snap_count, modes), jnp.bfloat16),
            pltpu.VMEM((freq_count, 2, 2 * snap_count, modes), jnp.float32),
            pltpu.VMEM((freq_count, ranges, depth_count), jnp.float32),
            pltpu.VMEM((ranges, 1, depth_count), jnp.float32),
            pltpu.VMEM((ranges, 1, depth_count), jnp.float32),
            pltpu.SemaphoreType.DMA((2,)),
            pltpu.SemaphoreType.DMA((freq_count,)),
            pltpu.SemaphoreType.DMA((freq_count,)),
            pltpu.SemaphoreType.DMA((freq_count,)),
            pltpu.SemaphoreType.DMA((groups,)),
            pltpu.SemaphoreType.DMA((groups,)),
            pltpu.SemaphoreType.DMA((ranges,)),
            pltpu.SemaphoreType.DMA((ranges,)),
        ],
        compiler_params=pltpu.CompilerParams(
            collective_id=0, has_side_effects=True, vmem_limit_bytes=56 * 1024 * 1024
        ),
    )(mode_counts, *inputs)
    return surface.reshape(1, tiles * depth_count)


def solution(mesh):
    in_specs = (
        P("freq", None, None, None),
        P(("groups", "freq"), None, None, None),
        P("freq", None),
        P("freq"),
        P("freq", None, None),
        P("freq", "tile", None),
    )
    out_specs = P(("groups", "tile", "freq"), None)
    return jax.shard_map(
        on_device, mesh=mesh, in_specs=in_specs, out_specs=out_specs, check_vma=False
    )
```

```python
import functools

import jax
import jax.numpy as jnp
from jax import lax
from jax.experimental import pallas as pl
from jax.experimental.pallas import tpu as pltpu
from jax.sharding import PartitionSpec as P

MBLK = 128
ZBLK = 32
MESH = pl.DeviceIdType.MESH

range_anchor = 1000.0
range_step = 25.0


def cosine_and_sine(angle):
    turns = jnp.floor(angle * 0.6366197723675814 + 0.5)
    rest = ((angle - turns * 1.5703125) - turns * 4.837512969970703125e-4) - (
        turns * 7.54978995489188216e-8
    )
    quarter = turns.astype(jnp.int32)
    square = rest * rest
    sine = rest + rest * square * (
        -1.6666654611e-1 + square * (8.3321608736e-3 - square * 1.9515295891e-4)
    )
    cosine = (1.0 - 0.5 * square) + square * square * (
        4.166664568298827e-2
        + square * (-1.388731625493765e-3 + square * 2.443315711809948e-5)
    )
    odd = (quarter & 1) == 1
    first = jnp.where(odd, sine, cosine)
    second = jnp.where(odd, cosine, sine)
    first = jnp.where(((quarter + 1) & 2) == 2, -first, first)
    second = jnp.where((quarter & 2) == 2, -second, second)
    return first, second


def surface_kernel(
    sizes,
    all_freqs,
    counts,
    mask_hbm,
    panels_hbm,
    snaps_hbm,
    wavenumbers_hbm,
    shapes_hbm,
    out,
    mask,
    panels,
    snaps,
    wavenumbers,
    shapes,
    cosines,
    sines,
    lhs_a,
    lhs_b,
    weights,
    energy,
    probe,
    panel_probe,
    power,
    rows_out,
    rows_in,
    table_sem,
    panel_sem,
    snap_sem,
    shape_sem,
    energy_send,
    energy_recv,
    row_send,
    row_recv,
):
    groups, tiles, freqs = sizes
    freq_count, depth_count, modes = shapes.shape
    receivers = panels.shape[2]
    snap_count = snaps.shape[2]
    ranges = rows_in.shape[0]
    table_rows = cosines.shape[1]
    own_ranges = ranges // groups
    per = min(4, own_ranges // 2)
    turns = own_ranges // 2 // per
    chunk = receivers // turns
    group = lax.axis_index("groups")
    tile = lax.axis_index("tile")
    freq = lax.axis_index("freq")
    peers = tiles * freqs
    me = tile * freqs + freq

    number_copy = pltpu.make_async_copy(wavenumbers_hbm, wavenumbers, table_sem.at[0])
    number_copy.start()
    panel_copies, snap_copies, shape_copies = [], [], []
    for f in range(freq_count):
        panel_copies.append(
            pltpu.make_async_copy(panels_hbm.at[f], panels.at[f], panel_sem.at[f])
        )
        shape_copies.append(
            pltpu.make_async_copy(shapes_hbm.at[f], shapes.at[f], shape_sem.at[f])
        )
        snap_copies.append(pltpu.make_async_copy(snaps_hbm.at[f], snaps.at[f], snap_sem.at[f]))
    mask_copy = pltpu.make_async_copy(mask_hbm, mask, table_sem.at[1])
    panel_copies[0].start()
    mask_copy.start()
    for f in range(freq_count):
        shape_copies[f].start()
        snap_copies[f].start()
        if f + 1 < freq_count:
            panel_copies[f + 1].start()

    barrier = pltpu.get_barrier_semaphore()
    for step in range(1, peers):
        other = lax.rem(me + step, peers)
        pl.semaphore_signal(
            barrier,
            inc=1,
            device_id=(group, lax.div(other, freqs), lax.rem(other, freqs)),
            device_id_type=MESH,
        )
    for step in range(1, groups):
        pl.semaphore_signal(
            barrier,
            inc=1,
            device_id=(lax.rem(group + step, groups), tile, freq),
            device_id_type=MESH,
        )

    number_copy.wait()
    pairs, all_pairs = own_ranges // 2, ranges // 2
    index = lax.broadcasted_iota(jnp.int32, (table_rows, modes), 0)
    away = range_step * (index.astype(jnp.float32) + 0.5)
    own_first = (group * own_ranges).astype(jnp.float32)
    own_middle = range_anchor + range_step * (own_first + 0.5 * (own_ranges - 1))
    all_middle = range_anchor + range_step * (0.5 * (ranges - 1))
    middle = jnp.where(index == all_pairs, own_middle, all_middle)
    distance = jnp.where(index < all_pairs, away, middle)
    for f in range(freq_count):
        c, s = cosine_and_sine(distance * wavenumbers[pl.ds(f, 1), :])
        for r in range(table_rows):
            cosines[f, r] = jnp.broadcast_to(c[r : r + 1, :], (8, modes))
            sines[f, r] = jnp.broadcast_to(s[r : r + 1, :], (8, modes))
    mask_copy.wait()

    block_count = mask.shape[2]
    depth_block = (
        lax.broadcasted_iota(jnp.int32, (block_count, depth_count), 1) + tile * depth_count
    ) // ZBLK
    one_hot = (
        depth_block == lax.broadcasted_iota(jnp.int32, (block_count, depth_count), 0)
    ).astype(jnp.bfloat16)
    mode_index = lax.broadcasted_iota(jnp.int32, (MBLK, depth_count), 0)

    def live_shapes(f):
        flags = mask[:, f, :].astype(jnp.float32).astype(jnp.bfloat16)
        live = jnp.dot(flags, one_hot, preferred_element_type=jnp.float32)
        for block in range(modes // MBLK):
            columns = pl.ds(block * MBLK, MBLK)
            inside = (mode_index + block * MBLK) < counts[f]
            keep = jnp.where(inside, live[block : block + 1, :], 0.0).astype(jnp.bfloat16)
            weights[f, columns, :] = shapes[f, :, columns].T * keep

    buffers = (lhs_a, lhs_b)
    piece = 16

    def rotate(real, imag, f, row):
        c, s = cosines[f, row], sines[f, row]
        return real * c - imag * s, imag * c + real * s

    def scale(value, table):
        return (value * table).reshape(-1, modes).astype(jnp.bfloat16)

    def turn(f, buffer, lowest, count):
        for start in range(0, count, piece):
            base = lowest + start
            rows = [
                pl.ds(pl.multiple_of(part * receivers + base, piece), piece) for part in range(4)
            ]
            real = panels[f, 0, rows[0], :].astype(jnp.float32).reshape(-1, 8, modes)
            imag = panels[f, 1, rows[0], :].astype(jnp.float32).reshape(-1, 8, modes)
            real, imag = rotate(real, imag, f, all_pairs)
            for i in range(pairs):
                c, s = cosines[f, i], sines[f, i]
                buffer[i, rows[0], :] = scale(real, c)
                buffer[i, rows[1], :] = scale(imag, c)
                buffer[i, rows[2], :] = scale(real, s)
                buffer[i, rows[3], :] = scale(imag, s)

    def two_sides(product, count):
        even_real, even_imag = product[:count], product[count : 2 * count]
        odd_real, odd_imag = product[2 * count : 3 * count], product[3 * count :]
        beyond_real, beyond_imag = even_real - odd_imag, even_imag + odd_real
        before_real, before_imag = even_real + odd_imag, even_imag - odd_real
        beyond = beyond_real * beyond_real + beyond_imag * beyond_imag
        before = before_real * before_real + before_imag * before_imag
        return jnp.sum(beyond, axis=0, keepdims=True), jnp.sum(before, axis=0, keepdims=True)

    def measure_energy(f, buffer, j):
        left = buffer[pl.ds(j * per, per)].reshape(per * 4 * receivers, modes)
        product = jnp.dot(left, weights[f], preferred_element_type=jnp.float32)
        for i in range(per):
            lowest = i * 4 * receivers
            beyond, before = two_sides(product[lowest : lowest + 4 * receivers], receivers)
            step = j * per + i
            energy[group, f, pl.ds(pairs + step, 1), :] = beyond / receivers + 1e-6
            energy[group, f, pl.ds(pairs - 1 - step, 1), :] = before / receivers + 1e-6

    def project_panels(f):
        pair = snaps[f].reshape(2 * snap_count, receivers)
        for half in range(2):
            panel_probe[f, half] = jnp.dot(
                pair, panels[f, half], preferred_element_type=jnp.float32
            )

    def turn_probe(f, j):
        on_real, on_imag = panel_probe[f, 0], panel_probe[f, 1]
        real = (on_real[:snap_count] + on_imag[snap_count:]).reshape(-1, 8, modes)
        imag = (on_imag[:snap_count] - on_real[snap_count:]).reshape(-1, 8, modes)
        real, imag = rotate(real, imag, f, all_pairs + 1)
        for i in range(per * groups):
            step = j * per * groups + i
            c, s = cosines[f, step], sines[f, step]
            probe[f, step, pl.ds(0, snap_count), :] = scale(real, c)
            probe[f, step, pl.ds(snap_count, snap_count), :] = scale(imag, c)
            probe[f, step, pl.ds(2 * snap_count, snap_count), :] = scale(real, s)
            probe[f, step, pl.ds(3 * snap_count, snap_count), :] = scale(imag, s)

    part_rows = receivers // freq_count
    for f in range(freq_count):
        panel_copies[f].wait()
        shape_copies[f].wait()
        snap_copies[f].wait()
        live_shapes(f)
        project_panels(f)
        turn(0, buffers[0], f * part_rows, part_rows)

    for stage in range(1, freq_count + 1):

        def body(j, carry, stage=stage):
            measure_energy(stage - 1, buffers[(stage - 1) % 2], j)
            if stage < freq_count:
                turn(stage, buffers[stage % 2], j * chunk, chunk)
            turn_probe(stage - 1, j)
            return carry

        lax.fori_loop(0, turns, body, 0)

    pl.semaphore_wait(barrier, peers - 1 + groups - 1)
    energy_copies = []
    for step in range(1, groups):
        energy_copies.append(
            pltpu.make_async_remote_copy(
                src_ref=energy.at[group],
                dst_ref=energy.at[group],
                send_sem=energy_send.at[step],
                recv_sem=energy_recv.at[step],
                device_id=(lax.rem(group + step, groups), tile, freq),
                device_id_type=MESH,
            )
        )
    for copy in energy_copies:
        copy.start()

    for f in range(freq_count):
        left = probe[f].reshape(-1, modes)
        projected = jnp.dot(left, weights[f], preferred_element_type=jnp.float32)
        for i in range(all_pairs):
            lowest = i * 4 * snap_count
            beyond, before = two_sides(projected[lowest : lowest + 4 * snap_count], snap_count)
            power[f, pl.ds(all_pairs + i, 1), :] = beyond / snap_count
            power[f, pl.ds(all_pairs - 1 - i, 1), :] = before / snap_count

    for copy in energy_copies:
        copy.wait()
    for g in range(groups):
        part = jnp.zeros((own_ranges, depth_count), jnp.float32)
        for f in range(freq_count):
            part += power[f, pl.ds(g * own_ranges, own_ranges), :] / (
                2.0 * receivers * energy[g, f]
            )
        for r in range(own_ranges):
            rows_out[g * own_ranges + r] = part[r : r + 1, :]

    row_copies = []
    for step in range(1, peers):
        other = lax.rem(me + step, peers)
        row_copies.append(
            pltpu.make_async_remote_copy(
                src_ref=rows_out.at[other],
                dst_ref=rows_in.at[me],
                send_sem=row_send.at[step],
                recv_sem=row_recv.at[step],
                device_id=(group, lax.div(other, freqs), lax.rem(other, freqs)),
                device_id_type=MESH,
            )
        )
    for copy in row_copies:
        copy.start()
    rows_in[me] = rows_out[me]
    for copy in row_copies:
        copy.wait()
    for t in range(tiles):
        total = rows_in[t * freqs]
        for f in range(1, freqs):
            total += rows_in[t * freqs + f]
        out[t] = total / all_freqs


def on_device(panels, snapshots, wavenumbers, mode_counts, mode_mask, mode_shapes):
    groups, tiles, freqs = (lax.axis_size(name) for name in ("groups", "tile", "freq"))
    freq_count, depth_count, modes = mode_shapes.shape
    receivers = panels.shape[2]
    ranges = tiles * freqs
    own_ranges = ranges // groups
    snap_count = snapshots.shape[2]
    vmem = pl.BlockSpec(memory_space=pltpu.VMEM)
    smem = pl.BlockSpec(memory_space=pltpu.SMEM)
    hbm = pl.BlockSpec(memory_space=pltpu.HBM)
    by_block = jnp.swapaxes(mode_mask, 0, 1)
    inputs = (by_block, panels, snapshots, wavenumbers, mode_shapes)
    surface = pl.pallas_call(
        functools.partial(surface_kernel, (groups, tiles, freqs), freq_count * freqs),
        out_shape=jax.ShapeDtypeStruct((tiles, 1, depth_count), jnp.float32),
        in_specs=[smem] + [hbm] * 5,
        out_specs=vmem,
        scratch_shapes=[pltpu.VMEM(value.shape, value.dtype) for value in inputs]
        + [
            pltpu.VMEM((freq_count, ranges // 2 + 2, 8, modes), jnp.float32),
            pltpu.VMEM((freq_count, ranges // 2 + 2, 8, modes), jnp.float32),
            pltpu.VMEM((own_ranges // 2, 4 * receivers, modes), jnp.bfloat16),
            pltpu.VMEM((own_ranges // 2, 4 * receivers, modes), jnp.bfloat16),
            pltpu.VMEM((freq_count, modes, depth_count), jnp.bfloat16),
            pltpu.VMEM((groups, freq_count, own_ranges, depth_count), jnp.float32),
            pltpu.VMEM((freq_count, ranges // 2, 4 * snap_count, modes), jnp.bfloat16),
            pltpu.VMEM((freq_count, 2, 2 * snap_count, modes), jnp.float32),
            pltpu.VMEM((freq_count, ranges, depth_count), jnp.float32),
            pltpu.VMEM((ranges, 1, depth_count), jnp.float32),
            pltpu.VMEM((ranges, 1, depth_count), jnp.float32),
            pltpu.SemaphoreType.DMA((2,)),
            pltpu.SemaphoreType.DMA((freq_count,)),
            pltpu.SemaphoreType.DMA((freq_count,)),
            pltpu.SemaphoreType.DMA((freq_count,)),
            pltpu.SemaphoreType.DMA((groups,)),
            pltpu.SemaphoreType.DMA((groups,)),
            pltpu.SemaphoreType.DMA((ranges,)),
            pltpu.SemaphoreType.DMA((ranges,)),
        ],
        compiler_params=pltpu.CompilerParams(
            collective_id=0, has_side_effects=True, vmem_limit_bytes=56 * 1024 * 1024
        ),
    )(mode_counts, *inputs)
    return surface.reshape(1, tiles * depth_count)


def solution(mesh):
    in_specs = (
        P("freq", None, None, None),
        P(("groups", "freq"), None, None, None),
        P("freq", None),
        P("freq"),
        P("freq", None, None),
        P("freq", "tile", None),
    )
    out_specs = P(("groups", "tile", "freq"), None)
    return jax.shard_map(
        on_device, mesh=mesh, in_specs=in_specs, out_specs=out_specs, check_vma=False
    )
```
